32 devices in a mesh: gx: 4 (over y, core), gy: 8 (over z, x).
Axes of the slice: x: 2, y: 2, z: 4, core: 2. Of those that a mesh axis runs over, the one named last changes fastest.
Arguments:
- old_state: float32 [135, 8192], P(None, ('gx', 'gy')), as said below
- old_inverse: bfloat16 [135, 135, 8192], P(None, None, ('gx', 'gy'))
- old_start: int32 [32], replicated, may hold values from 0 to 5984, as said below
- neighbours: int32 [6, 6144], P(None, ('gx', 'gy')), may hold values from 0 to 6143, as said below
- orientation: int32 [6, 6144], P(None, ('gx', 'gy')), may hold values from 0 to 7, as said below
Outputs:
- new_state: float32 [135, 6144], P(None, ('gx', 'gy'))
- residual: float32 [135, 6144], P(None, ('gx', 'gy'))
The draws below stay inside these ranges and needn't reach their ends.
Inputs may be any that keep to these rules, and one draw needn't show every extreme that they name: old_start[0] = 0 and each old_start[d] lies within 32 of d * 192; the last range ends at 6144; in every draw one device's old range holds exactly 256 elements, one start lies 32 below and another 32 above its new one, and the last start lies 32 above its new one. neighbours[f, e] names the element across face f of e; e is across face f xor 1 of that element. Device d holds elements d * 192 to (d + 1) * 192 - 1, with gx index d // 8 and gy index d % 8. The element across face 2k + h lies on e's own device, or for k = 0 on the device whose gx index is one lower (h = 0) or one higher (h = 1), cyclically, for k = 1 likewise along gy; for k = 2 it lies on e's own device. `orientation`: codes of the two sides of a face are inverse to one another. `old_state`: density lies in 0.5 to 1.8 and pressure in 0.5 to 1.8 at every node, padding slots included.
All inputs are finite; a program needn't handle non-finite values.
Results may differ from the reference program's by a relative error of at most 0.0003.
Values may be sent and summed in bfloat16 or wider, within the bound.
A program may use at most 128 MiB of HBM per device.

```python
import math
import jax
import jax.numpy as jnp
from jax import lax

BX = 4
BY = 4
BZ = 12
ELEM_DEV = 192
SHIFT = 32
CAPACITY = 256
ELEMS = 6144
N_GX = 4
N_GY = 8
DEVICES = 32


def mesh_tables(key):
    devices = N_GX * N_GY
    device_keys = jax.random.split(jax.random.fold_in(key, 11), devices)
    cell_orders = jax.vmap(lambda k: jax.random.permutation(k, ELEM_DEV))(device_keys).astype(jnp.int32)
    slot_of_cell = jax.vmap(lambda p: jnp.zeros_like(p).at[p].set(jnp.arange(ELEM_DEV, dtype=jnp.int32)))(cell_orders)
    device_ids = jnp.arange(devices, dtype=jnp.int32)[:, None]
    cell_x = cell_orders // (BY * BZ) + device_ids // N_GY * BX
    cell_y = cell_orders // BZ % BY + device_ids % N_GY * BY
    cell_z = cell_orders % BZ
    extents = [N_GX * BX, N_GY * BY, BZ]
    faces = []
    for face_id in range(6):
        offset_dir = 2 * (face_id % 2) - 1
        coords = [cell_x, cell_y, cell_z]
        coords[face_id // 2] = (coords[face_id // 2] + offset_dir) % extents[face_id // 2]
        owner_dev = coords[0] // BX * N_GY + coords[1] // BY
        target_cell = coords[0] % BX * (BY * BZ) + coords[1] % BY * BZ + coords[2]
        target_slot = slot_of_cell[owner_dev, target_cell]
        faces.append((owner_dev * ELEM_DEV + target_slot).reshape(-1))
    neighbours = jnp.stack(faces).astype(jnp.int32)
    plus_codes = jax.random.randint(jax.random.fold_in(key, 12), (3, devices * ELEM_DEV), 0, 8).astype(jnp.int32)
    codes = []
    for face_id in range(6):
        if face_id % 2 == 1:
            codes.append(plus_codes[face_id // 2])
        else:
            facing = jnp.take(plus_codes[face_id // 2], neighbours[face_id])
            low_bit = facing % 2
            mid_bit = facing // 2 % 2
            codes.append(jnp.where(facing >= 4, 4 + 2 * low_bit + mid_bit, facing))
    return (neighbours, jnp.stack(codes).astype(jnp.int32))


def draw_neighbours(key, part):
    shared = mesh_tables(key)
    return shared[0]


def draw_orientation(key, part):
    shared = mesh_tables(key)
    return shared[1]


def draw_old_start(key, part):
    key = jax.random.fold_in(key, 5)
    devices = N_GX * N_GY
    offsets = jax.random.randint(jax.random.fold_in(key, 1), (devices,), -SHIFT, SHIFT + 1).astype(jnp.int32)
    chosen = jax.random.randint(jax.random.fold_in(key, 2), (), 1, devices - 1).astype(jnp.int32)
    device_ids = jnp.arange(devices, dtype=jnp.int32)
    offsets = jnp.where(device_ids == chosen, -SHIFT, offsets)
    offsets = jnp.where(device_ids == chosen + 1, SHIFT, offsets)
    offsets = jnp.where(device_ids == devices - 1, SHIFT, offsets)
    offsets = jnp.where(device_ids == 0, 0, offsets)
    return (device_ids * ELEM_DEV + offsets).astype(jnp.int32)


def draw_old_state(key, part):
    key = jax.random.fold_in(key, 7)
    columns = CAPACITY * N_GX * N_GY
    array_shape = (27, columns)
    density = jnp.exp(jax.random.uniform(jax.random.fold_in(key, 1), array_shape, minval=math.log(0.6), maxval=math.log(1.6)))
    pressure = jnp.exp(jax.random.uniform(jax.random.fold_in(key, 2), array_shape, minval=math.log(0.6), maxval=math.log(1.6)))
    velocity = 0.3 * jnp.clip(jax.random.normal(jax.random.fold_in(key, 3), (3,) + array_shape), -3.0, 3.0)
    energy = pressure / 0.4 + 0.5 * density * jnp.sum(velocity * velocity, axis=0)
    stacked = jnp.concatenate([density[None], density[None] * velocity, energy[None]], axis=0)
    return stacked.reshape(135, columns).astype(jnp.float32)


def draw_old_inverse(key, part):
    key = jax.random.fold_in(key, 9)
    columns = CAPACITY * N_GX * N_GY
    on_diag = (jnp.arange(135)[:, None] == jnp.arange(135)[None, :])[:, :, None]
    diagonal = jnp.exp(jax.random.uniform(jax.random.fold_in(key, 1), (135, 1, columns), minval=math.log(0.05), maxval=math.log(0.2)))
    spread = jax.random.normal(jax.random.fold_in(key, 2), (135, 135, columns))
    off_diag = spread * (0.06 / math.sqrt(135.0))
    return jnp.where(on_diag, diagonal, off_diag).astype(jnp.bfloat16)


def setup_inputs(seed: int = 0) -> dict:
    key_of = jax.random.split(jax.random.key(seed), 6)
    return {
        "old_state": draw_old_state(jax.random.fold_in(key_of[5], 71), 0),
        "old_inverse": draw_old_inverse(jax.random.fold_in(key_of[5], 71), 0),
        "old_start": draw_old_start(jax.random.fold_in(key_of[5], 71), 0),
        "neighbours": draw_neighbours(jax.random.fold_in(key_of[5], 71), 0),
        "orientation": draw_orientation(jax.random.fold_in(key_of[5], 71), 0),
    }


DIFF = [[-1.5, 2.0, -0.5], [-0.5, 0.0, 0.5], [0.5, -2.0, 1.5]]

def face_orderings():
    layout = [[p * 3 + q for q in range(3)] for p in range(3)]
    orderings = []
    for variant in range(8):
        arranged = layout
        if variant >= 4:
            arranged = [[layout[q][p] for q in range(3)] for p in range(3)]
        if variant % 2 == 1:
            arranged = arranged[::-1]
        if variant // 2 % 2 == 1:
            arranged = [entries[::-1] for entries in arranged]
        orderings.append([arranged[p][q] for p in range(3) for q in range(3)])
    return orderings

def reorient(neighbour_trace, orient_codes):
    result = jnp.zeros_like(neighbour_trace)
    for variant, ordering in enumerate(face_orderings()):
        result = result + jnp.where(orient_codes == variant, neighbour_trace[:, ordering, :], 0.0)
    return result

def euler_flux(conserved, axis_dim):
    density = conserved[0]
    velocity = conserved[1:4] / density
    pressure = 0.4 * (conserved[4] - 0.5 * lax.optimization_barrier(jnp.sum(conserved[1:4] * velocity, axis=0)))
    normal_vel = velocity[axis_dim]
    momentum = [conserved[1 + k] * normal_vel for k in range(3)]
    momentum[axis_dim] = momentum[axis_dim] + pressure
    fluxes = jnp.stack([conserved[1 + axis_dim]] + momentum + [(conserved[4] + pressure) * normal_vel])
    speed = jnp.abs(normal_vel) + jnp.sqrt(1.4 * pressure / density)
    return (fluxes, speed)

def derivative(values, axis_pos):
    planes = [lax.index_in_dim(values, j, axis_pos, keepdims=False) for j in range(3)]
    derived = [DIFF[i][0] * planes[0] + DIFF[i][1] * planes[1] + DIFF[i][2] * planes[2] for i in range(3)]
    return jnp.stack(derived, axis=axis_pos)

def face_traces(conserved):
    columns = conserved.shape[-1]
    traces = []
    for face_id in range(6):
        traces.append(lax.index_in_dim(conserved, 2 * (face_id % 2), face_id // 2 + 1, keepdims=False).reshape(5, 9, columns))
    return jnp.stack(traces)

def dg_residual(flat, beyond):
    columns = flat.shape[-1]
    conserved = flat.reshape(5, 3, 3, 3, columns)
    residual = jnp.zeros_like(conserved)
    for axis_dim in range(3):
        residual = residual + derivative(euler_flux(conserved, axis_dim)[0], axis_dim + 1)
    for face_id in range(6):
        axis_dim = face_id // 2
        high_side = face_id % 2
        outward = 2.0 * high_side - 1.0
        inside = lax.index_in_dim(conserved, 2 * high_side, axis_dim + 1, keepdims=False)
        outside = beyond[face_id].reshape(inside.shape)
        flux_in, speed_in = euler_flux(inside, axis_dim)
        flux_out, speed_out = euler_flux(outside, axis_dim)
        wave_speed = jnp.maximum(speed_in, speed_out)
        common_flux = 0.5 * outward * (flux_in + flux_out) - 0.5 * wave_speed * (outside - inside)
        face_term = 3.0 * (common_flux - outward * flux_in)
        position = [slice(None)] * 5
        position[axis_dim + 1] = 2 * high_side
        residual = residual.at[tuple(position)].add(face_term)
    return residual.reshape(135, columns)

def old_columns(old_start, wanted):
    old_owner = (jnp.searchsorted(old_start, wanted, side='right') - 1).astype(jnp.int32)
    return (old_owner * CAPACITY + wanted - old_start[old_owner]).astype(jnp.int32)

def reference(old_state, old_inverse, old_start, neighbours, orientation):
    wanted = jnp.arange(ELEMS, dtype=jnp.int32)
    conserved = jnp.take(old_state, old_columns(old_start, wanted), axis=1)
    traces = face_traces(conserved.reshape(5, 3, 3, 3, ELEMS))
    beyond = [reorient(jnp.take(traces[face_id ^ 1], neighbours[face_id], axis=2), orientation[face_id]) for face_id in range(6)]
    residual = dg_residual(conserved, beyond)

    def block_update(block_id):
        block_elems = block_id * ELEM_DEV + jnp.arange(ELEM_DEV, dtype=jnp.int32)
        inverse = jnp.take(old_inverse, old_columns(old_start, block_elems), axis=2).astype(jnp.float32)
        block_rows = lax.dynamic_slice_in_dim(residual, block_id * ELEM_DEV, ELEM_DEV, 1)
        return jnp.einsum('ije,je->ie', inverse, block_rows, precision=lax.Precision.HIGHEST)
    update = lax.map(block_update, jnp.arange(DEVICES, dtype=jnp.int32))
    update = jnp.moveaxis(update, 0, 1).reshape(135, ELEMS)
    return (conserved - update, residual)
```

```python
import numpy as np
import jax
import jax.numpy as jnp
from jax import lax
from jax.experimental import pallas as pl
from jax.experimental.pallas import tpu as pltpu
from jax.sharding import PartitionSpec as P

DIFF = np.array([[-1.5, 2.0, -0.5], [-0.5, 0.0, 0.5], [0.5, -2.0, 1.5]])
MESH = pl.DeviceIdType.MESH
NODES = 27
ROWS = 135
FACE_ROWS = 48
CHUNKS = 5


def face_node(face, position):
    k, h = face // 2, face % 2
    other = [position // 3, position % 3]
    index = other[:k] + [2 * h] + other[k:]
    return 9 * index[0] + 3 * index[1] + index[2]


def selections():
    send = np.zeros((6 * FACE_ROWS, ROWS), np.float32)
    inside = np.zeros((72, NODES), np.float32)
    lift = np.zeros((NODES, 72), np.float32)
    for face in range(6):
        for position in range(9):
            node = face_node(face, position)
            for v in range(5):
                send[face * FACE_ROWS + v * 9 + position, v * NODES + node] = 1.0
            inside[position * 8 + face, node] = 1.0
            lift[node, position * 8 + face] = 1.0
    eye = np.eye(3)
    along = np.concatenate(
        [
            np.kron(np.kron(DIFF, eye), eye),
            np.kron(np.kron(eye, DIFF), eye),
            np.kron(np.kron(eye, eye), DIFF),
        ],
        axis=1,
    ).astype(np.float32)
    thrice = lambda m: np.concatenate([m, m, m], axis=1)
    return [jnp.asarray(thrice(m), jnp.bfloat16) for m in (send, inside, along, lift)]


def parts_of(x):
    high = x.astype(jnp.bfloat16)
    rest = x - high.astype(jnp.float32)
    mid = rest.astype(jnp.bfloat16)
    low = (rest - mid.astype(jnp.float32)).astype(jnp.bfloat16)
    return [high, mid, low]


def times(matrix, x):
    return jnp.dot(
        matrix, jnp.concatenate(parts_of(x), axis=0), preferred_element_type=jnp.float32
    )


def pressure_of(u, inverse_density):
    kinetic = (u[1] * u[1] + u[2] * u[2] + u[3] * u[3]) * inverse_density
    return 0.4 * (u[4] - 0.5 * kinetic)


def kernel(
    n_gx, n_gy,
    state_ref, inverse_ref, start_ref, neigh_ref, orient_ref,
    send_mat, inside_mat, along_mat, lift_mat,
    new_ref, residual_ref,
    block_ref, view_ref, edge_prev, edge_next,
    traces_ref, far_ref, out_ref, res_ref, res_prev, res_next,
    old_res, upd_ref, upd_prev, upd_next, index_ref, code_ref,
    load_sem, send_sem, recv_sem,
):
    elems = neigh_ref.shape[1]
    capacity = state_ref.shape[1]
    half = capacity // 2
    count = n_gx * n_gy
    gx = lax.axis_index("gx")
    gy = lax.axis_index("gy")
    me = gx * n_gy + gy

    after = lax.rem(me + 1, count)
    before = lax.rem(me + count - 1, count)
    nxt = (after // n_gy, lax.rem(after, n_gy))
    prv = (before // n_gy, lax.rem(before, n_gy))
    sides = [
        (lax.rem(gx + n_gx - 1, n_gx), gy),
        (lax.rem(gx + 1, n_gx), gy),
        (gx, lax.rem(gy + n_gy - 1, n_gy)),
        (gx, lax.rem(gy + 1, n_gy)),
    ]

    barrier = pltpu.get_barrier_semaphore()
    for device in [nxt, prv] + sides:
        pl.semaphore_signal(barrier, inc=1, device_id=device, device_id_type=MESH)

    rows = ROWS // CHUNKS
    loads = []
    for chunk in range(CHUNKS):
        where = pl.ds(chunk * rows, rows)
        load = pltpu.make_async_copy(
            inverse_ref.at[where], block_ref.at[where], load_sem.at[chunk]
        )
        load.start()
        loads.append(load)

    def send(slot, source, target, device):
        copy = pltpu.make_async_remote_copy(
            src_ref=source, dst_ref=target, send_sem=send_sem.at[slot],
            recv_sem=recv_sem.at[slot], device_id=device, device_id_type=MESH,
        )
        copy.start()
        return copy

    start = start_ref[me]
    end = jnp.where(me == count - 1, count * elems, start_ref[lax.rem(me + 1, count)])
    held = end - start
    shift = me * elems - start
    to_new = jnp.where(shift > 0, capacity - shift, -shift)
    to_old = jnp.where(shift >= 0, shift, capacity + shift)

    view_ref[...] = pltpu.roll(state_ref[...], to_new, 1)
    pl.semaphore_wait(barrier, 6)
    edge = view_ref.at[:, pl.ds(half, half)]
    copies = [send(0, edge, edge_prev, nxt), send(1, edge, edge_next, prv)]

    index_ref[...] = jnp.zeros_like(index_ref)
    code_ref[...] = jnp.zeros_like(code_ref)
    index_ref[0:6, 0:elems] = neigh_ref[...]
    code_ref[0:6, 0:elems] = orient_ref[...]
    choices = []
    for face in range(6):
        local = index_ref[face : face + 1, :] - me * elems
        if face < 4:
            own = jnp.logical_and(local >= 0, local < elems)
            other = sides[face][0] * n_gy + sides[face][1]
            local = jnp.where(own, local, capacity + local + (me - other) * elems)
        width = capacity * (2 if face < 4 else 1)
        columns = lax.broadcasted_iota(jnp.int32, (width, capacity), 0)
        choices.append(jnp.where(columns == local, 1.0, 0.0).astype(jnp.bfloat16))

    lane = lax.broadcasted_iota(jnp.int32, (1, half), 1)

    def merged(ref, from_prev, from_next):
        low = jnp.where(lane + shift < 0, pltpu.roll(from_prev[...], half // 2, 1), ref[:, 0:half])
        high = jnp.where(
            lane + half + shift >= held, pltpu.roll(from_next[...], half // 2, 1), ref[:, half:]
        )
        return low, high

    for copy in copies:
        copy.wait()
    low, high = merged(view_ref, edge_prev, edge_next)
    high = jnp.where(lane + half < elems, high, 0.0)
    view_ref[:, 0:half] = low
    view_ref[:, half:] = high
    state = view_ref[...]

    traces_ref[...] = times(send_mat[...], state)
    copies = []
    for face in range(4):
        copies.append(
            send(
                2 + face,
                traces_ref.at[pl.ds(face * FACE_ROWS, FACE_ROWS)],
                far_ref.at[pl.ds(face * FACE_ROWS, FACE_ROWS)],
                sides[face],
            )
        )

    u = [view_ref[NODES * v : NODES * (v + 1), :] for v in range(5)]
    inverse_density = 1.0 / u[0]
    pressure = pressure_of(u, inverse_density)
    flux = [[] for _ in range(5)]
    for k in range(3):
        velocity = u[1 + k] * inverse_density
        flux[0].append(u[1 + k])
        for j in range(3):
            value = u[1 + j] * velocity
            flux[1 + j].append(value + pressure if j == k else value)
        flux[4].append((u[4] + pressure) * velocity)
    volume = [times(along_mat[...], jnp.concatenate(flux[v], axis=0)) for v in range(5)]
    inside = [times(inside_mat[...], u[v]).reshape(9, 8, capacity) for v in range(5)]

    for face in range(4):
        copies[face].wait()

    out_ref[...] = jnp.zeros_like(out_ref)
    for face in range(6):
        where = pl.ds((face ^ 1) * FACE_ROWS, FACE_ROWS)
        block = traces_ref[where, :]
        if face < 4:
            block = jnp.concatenate([block, far_ref[where, :]], axis=1)
        pieces = jnp.dot(
            jnp.concatenate(parts_of(block), axis=0), choices[face],
            preferred_element_type=jnp.float32,
        )
        taken = pieces[0:48] + pieces[48:96] + pieces[96:144]
        out_ref[:, face, :] = taken[0:45]

    code = code_ref[...]
    swapped = code >= 4
    flip_p = (code & 1) == 1
    flip_q = (code & 2) == 2
    outside = []
    for v in range(5):
        t = [[out_ref[9 * v + 3 * p + q] for q in range(3)] for p in range(3)]
        t = [[jnp.where(swapped, t[q][p], t[p][q]) if p != q else t[p][q] for q in range(3)] for p in range(3)]
        t = [[jnp.where(flip_p, t[2 - p][q], t[p][q]) if p != 1 else t[p][q] for q in range(3)] for p in range(3)]
        t = [[jnp.where(flip_q, t[p][2 - q], t[p][q]) if q != 1 else t[p][q] for q in range(3)] for p in range(3)]
        outside.append(jnp.stack([t[p][q] for p in range(3) for q in range(3)]))

    face_of = lax.broadcasted_iota(jnp.int32, (1, 8, capacity), 1)
    real = face_of < 6
    outward = jnp.where((face_of & 1) == 1, 1.0, -1.0)
    normal = [jnp.logical_and(face_of >= 2 * k, face_of < 2 * k + 2) for k in range(3)]

    def normal_flux(w):
        inverse_density = 1.0 / w[0]
        pressure = pressure_of(w, inverse_density)
        momentum = jnp.where(normal[0], w[1], jnp.where(normal[1], w[2], w[3]))
        velocity = momentum * inverse_density
        values = [momentum]
        for j in range(3):
            values.append(w[1 + j] * velocity + jnp.where(normal[j], pressure, 0.0))
        values.append((w[4] + pressure) * velocity)
        return values, jnp.abs(velocity) + jnp.sqrt(1.4 * pressure * inverse_density)

    flux_in, speed_in = normal_flux(inside)
    flux_out, speed_out = normal_flux(outside)
    speed = jnp.maximum(speed_in, speed_out)
    for v in range(5):
        term = 1.5 * (outward * (flux_out[v] - flux_in[v]) - speed * (outside[v] - inside[v]))
        term = jnp.where(real, term, 0.0).reshape(72, capacity)
        res_ref[NODES * v : NODES * (v + 1), :] = volume[v] + times(lift_mat[...], term)

    copies = [
        send(6, res_ref.at[:, pl.ds(0, half)], res_next, prv),
        send(7, res_ref.at[:, pl.ds(half, half)], res_prev, nxt),
    ]
    residual_ref[...] = res_ref[:, 0:elems]
    for copy in copies:
        copy.wait()
    quarter = half // 2
    inner = lane < elems - half
    to_next = lane < elems - half + quarter // 2
    high = jnp.where(
        inner, res_ref[:, half:],
        jnp.where(to_next, pltpu.roll(res_next[...], quarter, 1), pltpu.roll(res_prev[...], quarter, 1)),
    )
    old_res[...] = pltpu.roll(jnp.concatenate([res_ref[:, 0:half], high], axis=1), to_old, 1)

    for chunk in range(CHUNKS):
        loads[chunk].wait()

        def apply(step, carry):
            for t in range(3):
                row = chunk * rows + step * 3 + t
                product = block_ref[row].astype(jnp.float32) * old_res[...]
                upd_ref[pl.ds(row, 1), :] = jnp.sum(product, axis=0, keepdims=True)
            return carry

        lax.fori_loop(0, rows // 3, apply, 0)

    upd_ref[...] = pltpu.roll(upd_ref[...], to_new, 1)
    edge = upd_ref.at[:, pl.ds(half, half)]
    copies = [send(8, edge, upd_prev, nxt), send(9, edge, upd_next, prv)]
    for copy in copies:
        copy.wait()
    low, high = merged(upd_ref, upd_prev, upd_next)
    new_ref[:, 0:half] = view_ref[:, 0:half] - low
    new_ref[:, half:elems] = (view_ref[:, half:] - high)[:, 0 : elems - half]


def solution(mesh):
    n_gx, n_gy = mesh.shape["gx"], mesh.shape["gy"]

    def body(old_state, old_inverse, old_start, neighbours, orientation):
        elems, capacity = neighbours.shape[1], old_state.shape[1]
        half = capacity // 2
        vmem = pl.BlockSpec(memory_space=pltpu.VMEM)
        f32 = lambda *shape: pltpu.VMEM(shape, jnp.float32)
        call = pl.pallas_call(
            lambda *refs: kernel(n_gx, n_gy, *refs),
            out_shape=[jax.ShapeDtypeStruct((ROWS, elems), jnp.float32)] * 2,
            in_specs=[
                vmem,
                pl.BlockSpec(memory_space=pl.ANY),
                pl.BlockSpec(memory_space=pltpu.SMEM),
                vmem, vmem, vmem, vmem, vmem, vmem,
            ],
            out_specs=[vmem, vmem],
            scratch_shapes=[
                pltpu.VMEM((ROWS, ROWS, capacity), jnp.bfloat16),
                f32(ROWS, capacity), f32(ROWS, half), f32(ROWS, half),
                f32(6 * FACE_ROWS, capacity), f32(4 * FACE_ROWS, capacity),
                f32(45, 8, capacity),
                f32(ROWS, capacity), f32(ROWS, half), f32(ROWS, half),
                f32(ROWS, capacity),
                f32(ROWS, capacity), f32(ROWS, half), f32(ROWS, half),
                pltpu.VMEM((8, capacity), jnp.int32), pltpu.VMEM((8, capacity), jnp.int32),
                pltpu.SemaphoreType.DMA((CHUNKS,)),
                pltpu.SemaphoreType.DMA((10,)),
                pltpu.SemaphoreType.DMA((10,)),
            ],
            compiler_params=pltpu.CompilerParams(
                collective_id=0, has_side_effects=True, vmem_limit_bytes=48 * 1024 * 1024
            ),
        )
        return tuple(call(old_state, old_inverse, old_start, neighbours, orientation, *selections()))

    spread = P(None, ("gx", "gy"))
    return jax.shard_map(
        body,
        mesh=mesh,
        in_specs=(spread, P(None, None, ("gx", "gy")), P(), spread, spread),
        out_specs=(spread, spread),
        check_vma=False,
    )
```

```python
import numpy as np
import jax
import jax.numpy as jnp
from jax import lax
from jax.experimental import pallas as pl
from jax.experimental.pallas import tpu as pltpu
from jax.sharding import PartitionSpec as P

DIFF = np.array([[-1.5, 2.0, -0.5], [-0.5, 0.0, 0.5], [0.5, -2.0, 1.5]])
MESH = pl.DeviceIdType.MESH
NODES = 27
ROWS = 135
FACE_ROWS = 48
CHUNKS = 5


def face_node(face, position):
    k, h = face // 2, face % 2
    other = [position // 3, position % 3]
    index = other[:k] + [2 * h] + other[k:]
    return 9 * index[0] + 3 * index[1] + index[2]


def selections():
    send = np.zeros((6 * FACE_ROWS, ROWS), np.float32)
    inside = np.zeros((80, NODES), np.float32)
    lift = np.zeros((32, 72), np.float32)
    for face in range(6):
        for position in range(9):
            node = face_node(face, position)
            for v in range(5):
                send[face * FACE_ROWS + v * 9 + position, v * NODES + node] = 1.0
            inside[position * 8 + face, node] = 1.0
            lift[node, position * 8 + face] = 1.0
    eye = np.eye(3)
    along = np.concatenate(
        [
            np.kron(np.kron(DIFF, eye), eye),
            np.kron(np.kron(eye, DIFF), eye),
            np.kron(np.kron(eye, eye), DIFF),
        ],
        axis=1,
    ).astype(np.float32)
    along = np.pad(along, ((0, 5), (0, 0)))
    thrice = lambda m: np.concatenate([m, m, m], axis=1)
    return [jnp.asarray(thrice(m), jnp.bfloat16) for m in (send, inside, along, lift)]


def parts_of(x):
    high = x.astype(jnp.bfloat16)
    rest = x - high.astype(jnp.float32)
    mid = rest.astype(jnp.bfloat16)
    low = (rest - mid.astype(jnp.float32)).astype(jnp.bfloat16)
    return [high, mid, low]


def times(matrix, x):
    return jnp.dot(
        matrix, jnp.concatenate(parts_of(x), axis=0), preferred_element_type=jnp.float32
    )


def pressure_of(u, inverse_density):
    kinetic = (u[1] * u[1] + u[2] * u[2] + u[3] * u[3]) * inverse_density
    return 0.4 * (u[4] - 0.5 * kinetic)


def kernel(
    n_gx, n_gy,
    state_hbm, inverse_ref, start_hbm, neigh_hbm, orient_hbm, send_hbm, inside_hbm, along_hbm, lift_hbm,
    new_ref, residual_ref,
    state_ref, start_ref, neigh_ref, orient_ref, send_mat, inside_mat, along_mat, lift_mat,
    block_ref, view_ref, edge_prev, edge_next,
    raw_ref, traces_ref, far_ref, far_prev, far_next, out_ref, res_ref, res_prev, res_next,
    old_res, upd_ref, upd_prev, upd_next, index_ref, code_ref,
    input_sem, load_sem, send_sem, recv_sem,
):
    elems = neigh_ref.shape[1]
    capacity = state_ref.shape[1]
    half = capacity // 2
    count = n_gx * n_gy
    gx = lax.axis_index("gx")
    gy = lax.axis_index("gy")
    me = gx * n_gy + gy

    after = lax.rem(me + 1, count)
    before = lax.rem(me + count - 1, count)
    def coords(device):
        return (device // n_gy, lax.rem(device, n_gy))

    def side(face, device):
        x, y = coords(device)
        step = 1 if face % 2 else -1
        if face < 2:
            x = lax.rem(x + n_gx + step, n_gx)
        else:
            y = lax.rem(y + n_gy + step, n_gy)
        return x * n_gy + y

    nxt, prv = coords(after), coords(before)
    sides = [side(face, me) for face in range(4)]
    via_next = [side(face, after) for face in range(4)]
    via_prev = [side(face, before) for face in range(4)]

    inputs = []
    for slot, (source, target) in enumerate(
        [
            (state_hbm, state_ref), (start_hbm, start_ref), (send_hbm, send_mat),
            (neigh_hbm, neigh_ref), (orient_hbm, orient_ref), (inside_hbm, inside_mat),
            (along_hbm, along_mat), (lift_hbm, lift_mat),
        ]
    ):
        load = pltpu.make_async_copy(source, target, input_sem.at[slot])
        load.start()
        inputs.append(load)

    barrier = pltpu.get_barrier_semaphore()
    for device in [after, before] + sides:
        pl.semaphore_signal(barrier, inc=1, device_id=coords(device), device_id_type=MESH)
    expected = 6
    for face in range(4):
        for sender in (
            lax.rem(sides[face] + count - 1, count), lax.rem(sides[face] + 1, count)
        ):
            expected = expected + jnp.where(sender == me, 0, 1)

            @pl.when(sender != me)
            def _():
                pl.semaphore_signal(barrier, inc=1, device_id=coords(sender), device_id_type=MESH)

    rows = ROWS // CHUNKS
    loads = []
    for chunk in range(CHUNKS):
        where = pl.ds(chunk * rows, rows)
        load = pltpu.make_async_copy(
            inverse_ref.at[where], block_ref.at[where], load_sem.at[chunk]
        )
        load.start()
        loads.append(load)

    def send(slot, source, target, device):
        copy = pltpu.make_async_remote_copy(
            src_ref=source, dst_ref=target, send_sem=send_sem.at[slot],
            recv_sem=recv_sem.at[slot], device_id=device, device_id_type=MESH,
        )
        copy.start()
        return copy

    def post(slot, source, target, device):
        remote = pltpu.make_async_remote_copy(
            src_ref=source, dst_ref=target, send_sem=send_sem.at[slot],
            recv_sem=recv_sem.at[slot], device_id=coords(device), device_id_type=MESH,
        )
        local = pltpu.make_async_copy(source, target, recv_sem.at[slot])
        pl.when(device != me)(remote.start)
        pl.when(device == me)(local.start)
        return device, remote, local

    def arrive(posted):
        device, remote, local = posted
        pl.when(device != me)(remote.wait)
        pl.when(device == me)(local.wait)

    def range_of(device):
        start = start_ref[device]
        end = jnp.where(
            device == count - 1, count * elems, start_ref[lax.rem(device + 1, count)]
        )
        return device * elems - start, end - start

    for load in inputs[:3]:
        load.wait()
    shift, held = range_of(me)
    to_new = jnp.where(shift > 0, capacity - shift, -shift)
    to_old = jnp.where(shift >= 0, shift, capacity + shift)

    view_ref[...] = pltpu.roll(state_ref[...], to_new, 1)
    raw_ref[...] = times(send_mat[pl.ds(0, 4 * FACE_ROWS), :], view_ref[...])
    pl.semaphore_wait(barrier, expected)
    edge = view_ref.at[:, pl.ds(half, half)]
    posted = []
    for face in range(4):
        where = pl.ds(face * FACE_ROWS, FACE_ROWS)
        ends = raw_ref.at[where, pl.ds(half, half)]
        posted.append(post(6 + face, ends, far_prev.at[where], via_next[face]))
        posted.append(post(10 + face, ends, far_next.at[where], via_prev[face]))
    copies = [send(0, edge, edge_prev, nxt), send(1, edge, edge_next, prv)]
    for face in range(4):
        where = pl.ds(face * FACE_ROWS, FACE_ROWS)
        copies.append(send(2 + face, raw_ref.at[where], far_ref.at[where], coords(sides[face])))

    for load in inputs[3:]:
        load.wait()
    index_ref[...] = jnp.zeros_like(index_ref)
    code_ref[...] = jnp.zeros_like(code_ref)
    index_ref[0:6, 0:elems] = neigh_ref[...]
    code_ref[0:6, 0:elems] = orient_ref[...]
    choices = []
    for face in range(6):
        local = index_ref[face : face + 1, :] - me * elems
        if face < 4:
            own = jnp.logical_and(local >= 0, local < elems)
            local = jnp.where(own, local, capacity + local + (me - sides[face]) * elems)
        width = capacity * (2 if face < 4 else 1)
        columns = lax.broadcasted_iota(jnp.int32, (width, capacity), 0)
        choices.append(jnp.where(columns == local, 1.0, 0.0).astype(jnp.bfloat16))

    lane = lax.broadcasted_iota(jnp.int32, (1, half), 1)

    def merged(low, high, from_prev, from_next, shift, held):
        low = jnp.where(lane + shift < 0, pltpu.roll(from_prev, half // 2, 1), low)
        high = jnp.where(lane + half + shift >= held, pltpu.roll(from_next, half // 2, 1), high)
        return low, high

    for copy in copies[:2]:
        copy.wait()
    low, high = merged(
        view_ref[:, 0:half], view_ref[:, half:], edge_prev[...], edge_next[...], shift, held
    )
    view_ref[:, 0:half] = low
    view_ref[:, half:] = high
    state = view_ref[...]
    traces_ref[...] = times(send_mat[...], state)

    u = [view_ref[NODES * v : NODES * (v + 1), :] for v in range(5)]
    inverse_density = 1.0 / u[0]
    pressure = pressure_of(u, inverse_density)
    flux = [[] for _ in range(5)]
    for k in range(3):
        velocity = u[1 + k] * inverse_density
        flux[0].append(u[1 + k])
        for j in range(3):
            value = u[1 + j] * velocity
            flux[1 + j].append(value + pressure if j == k else value)
        flux[4].append((u[4] + pressure) * velocity)
    volume = [times(along_mat[...], jnp.concatenate(flux[v], axis=0))[0:NODES] for v in range(5)]
    inside = [times(inside_mat[...], u[v])[0:72].reshape(9, 8, capacity) for v in range(5)]

    for copy in copies[2:]:
        copy.wait()
    for item in posted:
        arrive(item)

    out_ref[...] = jnp.zeros_like(out_ref)
    for face in range(6):
        where = pl.ds((face ^ 1) * FACE_ROWS, FACE_ROWS)
        block = traces_ref[where, :]
        if face < 4:
            low, high = merged(
                far_ref[where, 0:half], far_ref[where, half:], far_prev[where, :],
                far_next[where, :], *range_of(sides[face]),
            )
            block = jnp.concatenate([block, low, high], axis=1)
        pieces = jnp.dot(
            jnp.concatenate(parts_of(block), axis=0), choices[face],
            preferred_element_type=jnp.float32,
        )
        taken = pieces[0:48] + pieces[48:96] + pieces[96:144]
        out_ref[:, face, :] = taken[0:45]

    code = code_ref[...]
    swapped = code >= 4
    flip_p = (code & 1) == 1
    flip_q = (code & 2) == 2
    outside = []
    for v in range(5):
        t = [[out_ref[9 * v + 3 * p + q] for q in range(3)] for p in range(3)]
        t = [[jnp.where(swapped, t[q][p], t[p][q]) if p != q else t[p][q] for q in range(3)] for p in range(3)]
        t = [[jnp.where(flip_p, t[2 - p][q], t[p][q]) if p != 1 else t[p][q] for q in range(3)] for p in range(3)]
        t = [[jnp.where(flip_q, t[p][2 - q], t[p][q]) if q != 1 else t[p][q] for q in range(3)] for p in range(3)]
        outside.append(jnp.stack([t[p][q] for p in range(3) for q in range(3)]))

    face_of = lax.broadcasted_iota(jnp.int32, (1, 8, capacity), 1)
    real = face_of < 6
    outward = jnp.where((face_of & 1) == 1, 1.0, -1.0)
    normal = [jnp.logical_and(face_of >= 2 * k, face_of < 2 * k + 2) for k in range(3)]

    def normal_flux(w):
        inverse_density = 1.0 / w[0]
        pressure = pressure_of(w, inverse_density)
        momentum = jnp.where(normal[0], w[1], jnp.where(normal[1], w[2], w[3]))
        velocity = momentum * inverse_density
        values = [momentum]
        for j in range(3):
            values.append(w[1 + j] * velocity + jnp.where(normal[j], pressure, 0.0))
        values.append((w[4] + pressure) * velocity)
        return values, jnp.abs(velocity) + jnp.sqrt(1.4 * pressure * inverse_density)

    flux_in, speed_in = normal_flux(inside)
    flux_out, speed_out = normal_flux(outside)
    speed = jnp.maximum(speed_in, speed_out)
    for v in range(5):
        term = 1.5 * (outward * (flux_out[v] - flux_in[v]) - speed * (outside[v] - inside[v]))
        term = jnp.where(real, term, 0.0).reshape(72, capacity)
        res_ref[NODES * v : NODES * (v + 1), :] = volume[v] + times(lift_mat[...], term)[0:NODES]

    copies = [
        send(14, res_ref.at[:, pl.ds(0, half)], res_next, prv),
        send(15, res_ref.at[:, pl.ds(half, half)], res_prev, nxt),
    ]
    residual_ref[...] = res_ref[:, 0:elems]
    for copy in copies:
        copy.wait()
    quarter = half // 2
    inner = lane < elems - half
    to_next = lane < elems - half + quarter // 2
    high = jnp.where(
        inner, res_ref[:, half:],
        jnp.where(to_next, pltpu.roll(res_next[...], quarter, 1), pltpu.roll(res_prev[...], quarter, 1)),
    )
    old_res[...] = pltpu.roll(jnp.concatenate([res_ref[:, 0:half], high], axis=1), to_old, 1)

    for chunk in range(CHUNKS):
        loads[chunk].wait()

        def apply(step, carry):
            for t in range(3):
                row = chunk * rows + step * 3 + t
                product = block_ref[row].astype(jnp.float32) * old_res[...]
                upd_ref[pl.ds(row, 1), :] = jnp.sum(product, axis=0, keepdims=True)
            return carry

        lax.fori_loop(0, rows // 3, apply, 0)

    upd_ref[...] = pltpu.roll(upd_ref[...], to_new, 1)
    edge = upd_ref.at[:, pl.ds(half, half)]
    copies = [send(16, edge, upd_prev, nxt), send(17, edge, upd_next, prv)]
    for copy in copies:
        copy.wait()
    low, high = merged(
        upd_ref[:, 0:half], upd_ref[:, half:], upd_prev[...], upd_next[...], shift, held
    )
    new_ref[:, 0:half] = view_ref[:, 0:half] - low
    new_ref[:, half:elems] = (view_ref[:, half:] - high)[:, 0 : elems - half]


def solution(mesh):
    n_gx, n_gy = mesh.shape["gx"], mesh.shape["gy"]

    def body(old_state, old_inverse, old_start, neighbours, orientation):
        elems, capacity = neighbours.shape[1], old_state.shape[1]
        half = capacity // 2
        matrices = selections()
        vmem = pl.BlockSpec(memory_space=pltpu.VMEM)
        f32 = lambda *shape: pltpu.VMEM(shape, jnp.float32)
        call = pl.pallas_call(
            lambda *refs: kernel(n_gx, n_gy, *refs),
            out_shape=[jax.ShapeDtypeStruct((ROWS, elems), jnp.float32)] * 2,
            in_specs=[pl.BlockSpec(memory_space=pltpu.HBM)] * 9,
            out_specs=[vmem, vmem],
            scratch_shapes=[
                f32(ROWS, capacity),
                pltpu.SMEM(old_start.shape, jnp.int32),
                pltpu.VMEM((6, elems), jnp.int32), pltpu.VMEM((6, elems), jnp.int32),
                *[pltpu.VMEM(m.shape, m.dtype) for m in matrices],
                pltpu.VMEM((ROWS, ROWS, capacity), jnp.bfloat16),
                f32(ROWS, capacity), f32(ROWS, half), f32(ROWS, half),
                f32(4 * FACE_ROWS, capacity), f32(6 * FACE_ROWS, capacity),
                f32(4 * FACE_ROWS, capacity), f32(4 * FACE_ROWS, half), f32(4 * FACE_ROWS, half),
                f32(45, 8, capacity),
                f32(ROWS, capacity), f32(ROWS, half), f32(ROWS, half),
                f32(ROWS, capacity),
                f32(ROWS, capacity), f32(ROWS, half), f32(ROWS, half),
                pltpu.VMEM((8, capacity), jnp.int32), pltpu.VMEM((8, capacity), jnp.int32),
                pltpu.SemaphoreType.DMA((8,)),
                pltpu.SemaphoreType.DMA((CHUNKS,)),
                pltpu.SemaphoreType.DMA((18,)),
                pltpu.SemaphoreType.DMA((18,)),
            ],
            compiler_params=pltpu.CompilerParams(
                collective_id=0, has_side_effects=True, vmem_limit_bytes=48 * 1024 * 1024
            ),
        )
        return tuple(call(old_state, old_inverse, old_start, neighbours, orientation, *matrices))

    spread = P(None, ("gx", "gy"))
    return jax.shard_map(
        body,
        mesh=mesh,
        in_specs=(spread, P(None, None, ("gx", "gy")), P(), spread, spread),
        out_specs=(spread, spread),
        check_vma=False,
    )
```

```python
import numpy as np
import jax
import jax.numpy as jnp
from jax import lax
from jax.experimental import pallas as pl
from jax.experimental.pallas import tpu as pltpu
from jax.sharding import PartitionSpec as P

DIFF = np.array([[-1.5, 2.0, -0.5], [-0.5, 0.0, 0.5], [0.5, -2.0, 1.5]])
MESH = pl.DeviceIdType.MESH
NODES = 27
ROWS = 135
FACE_ROWS = 48
CHUNKS = 5
TALL = 160
EDGE = 32


def face_node(face, position):
    k, h = face // 2, face % 2
    other = [position // 3, position % 3]
    index = other[:k] + [2 * h] + other[k:]
    return 9 * index[0] + 3 * index[1] + index[2]


def selections():
    send = np.zeros((6 * FACE_ROWS, ROWS), np.float32)
    inside = np.zeros((80, NODES), np.float32)
    lift = np.zeros((32, 72), np.float32)
    for face in range(6):
        for position in range(9):
            node = face_node(face, position)
            for v in range(5):
                send[face * FACE_ROWS + v * 9 + position, v * NODES + node] = 1.0
            inside[position * 8 + face, node] = 1.0
            lift[node, position * 8 + face] = 1.0
    eye = np.eye(3)
    along = np.concatenate(
        [
            np.kron(np.kron(DIFF, eye), eye),
            np.kron(np.kron(eye, DIFF), eye),
            np.kron(np.kron(eye, eye), DIFF),
        ],
        axis=1,
    ).astype(np.float32)
    along = np.pad(along, ((0, 5), (0, 0)))
    thrice = lambda m: np.concatenate([m, m, m], axis=1)
    return [jnp.asarray(thrice(m), jnp.bfloat16) for m in (send, inside, along, lift)]


def parts_of(x):
    high = x.astype(jnp.bfloat16)
    rest = x - high.astype(jnp.float32)
    mid = rest.astype(jnp.bfloat16)
    low = (rest - mid.astype(jnp.float32)).astype(jnp.bfloat16)
    return [high, mid, low]


def times(matrix, x):
    return jnp.dot(
        matrix, jnp.concatenate(parts_of(x), axis=0), preferred_element_type=jnp.float32
    )


def packed(x, first, height):
    lane = lax.broadcasted_iota(jnp.int32, (1, 128), 1)
    result = jnp.zeros((height, 128), x.dtype)
    for group in range(x.shape[0] // height):
        rolled = pltpu.roll(
            x[group * height : (group + 1) * height], (group * EDGE - first) % 128, 1
        )
        inside = jnp.logical_and(lane >= group * EDGE, lane < (group + 1) * EDGE)
        result = jnp.where(inside, rolled, result)
    return result


def unpacked(x, first, groups):
    return jnp.concatenate(
        [pltpu.roll(x, (first - group * EDGE) % 128, 1) for group in range(groups)], axis=0
    )


def pressure_of(u, inverse_density):
    kinetic = (u[1] * u[1] + u[2] * u[2] + u[3] * u[3]) * inverse_density
    return 0.4 * (u[4] - 0.5 * kinetic)


def kernel(
    n_gx, n_gy,
    state_hbm, inverse_ref, start_hbm, neigh_hbm, orient_hbm, send_hbm, inside_hbm, along_hbm, lift_hbm,
    new_ref, residual_ref,
    state_ref, start_ref, neigh_ref, orient_ref, send_mat, inside_mat, along_mat, lift_mat,
    block_ref, view_ref, to_prev, to_next, edge_prev, edge_next, raw_prev, raw_next,
    raw_ref, traces_ref, far_ref, far_prev, far_next, out_ref, res_ref, res_prev, res_next,
    old_res, upd_ref, upd_prev, upd_next, index_ref, code_ref,
    input_sem, load_sem, send_sem, recv_sem,
):
    elems = neigh_ref.shape[1]
    capacity = state_ref.shape[1]
    half = capacity // 2
    count = n_gx * n_gy
    gx = lax.axis_index("gx")
    gy = lax.axis_index("gy")
    me = gx * n_gy + gy

    after = lax.rem(me + 1, count)
    before = lax.rem(me + count - 1, count)
    def coords(device):
        return (device // n_gy, lax.rem(device, n_gy))

    def side(face, device):
        x, y = coords(device)
        step = 1 if face % 2 else -1
        if face < 2:
            x = lax.rem(x + n_gx + step, n_gx)
        else:
            y = lax.rem(y + n_gy + step, n_gy)
        return x * n_gy + y

    nxt, prv = coords(after), coords(before)
    sides = [side(face, me) for face in range(4)]
    via_next = [side(face, after) for face in range(4)]
    via_prev = [side(face, before) for face in range(4)]

    inputs = []
    for slot, (source, target) in enumerate(
        [
            (state_hbm, state_ref), (start_hbm, start_ref), (send_hbm, send_mat),
            (neigh_hbm, neigh_ref), (orient_hbm, orient_ref), (inside_hbm, inside_mat),
            (along_hbm, along_mat), (lift_hbm, lift_mat),
        ]
    ):
        load = pltpu.make_async_copy(source, target, input_sem.at[slot])
        load.start()
        inputs.append(load)

    barrier = pltpu.get_barrier_semaphore()
    for device in [after, before] + sides:
        pl.semaphore_signal(barrier, inc=1, device_id=coords(device), device_id_type=MESH)
    expected = 6
    for face in range(4):
        for sender in (
            lax.rem(sides[face] + count - 1, count), lax.rem(sides[face] + 1, count)
        ):
            expected = expected + jnp.where(sender == me, 0, 1)

            @pl.when(sender != me)
            def _():
                pl.semaphore_signal(barrier, inc=1, device_id=coords(sender), device_id_type=MESH)

    rows = ROWS // CHUNKS
    loads = []
    for chunk in range(CHUNKS):
        where = pl.ds(chunk * rows, rows)
        load = pltpu.make_async_copy(
            inverse_ref.at[where], block_ref.at[where], load_sem.at[chunk]
        )
        load.start()
        loads.append(load)

    def send(slot, source, target, device):
        copy = pltpu.make_async_remote_copy(
            src_ref=source, dst_ref=target, send_sem=send_sem.at[slot],
            recv_sem=recv_sem.at[slot], device_id=device, device_id_type=MESH,
        )
        copy.start()
        return copy

    def post(slot, source, target, device):
        remote = pltpu.make_async_remote_copy(
            src_ref=source, dst_ref=target, send_sem=send_sem.at[slot],
            recv_sem=recv_sem.at[slot], device_id=coords(device), device_id_type=MESH,
        )
        local = pltpu.make_async_copy(source, target, recv_sem.at[slot])
        pl.when(device != me)(remote.start)
        pl.when(device == me)(local.start)
        return device, remote, local

    def arrive(posted):
        device, remote, local = posted
        pl.when(device != me)(remote.wait)
        pl.when(device == me)(local.wait)

    def range_of(device):
        start = start_ref[device]
        end = jnp.where(
            device == count - 1, count * elems, start_ref[lax.rem(device + 1, count)]
        )
        return device * elems - start, end - start

    for load in inputs[:3]:
        load.wait()
    shift, held = range_of(me)
    to_new = jnp.where(shift > 0, capacity - shift, -shift)
    to_old = jnp.where(shift >= 0, shift, capacity + shift)

    for ref in (view_ref, res_ref, upd_ref):
        ref[ROWS:, :] = jnp.zeros((TALL - ROWS, capacity), jnp.float32)
    view_ref[0:ROWS, :] = pltpu.roll(state_ref[...], to_new, 1)
    to_next[0] = packed(view_ref[:, half:], half // 2, TALL // 4)
    to_prev[0] = packed(view_ref[:, half:], half // 2 + EDGE, TALL // 4)
    raw_ref[...] = times(send_mat[pl.ds(0, 4 * FACE_ROWS), :], view_ref[0:ROWS, :])
    for face in range(4):
        ends = raw_ref[face * FACE_ROWS : (face + 1) * FACE_ROWS, half:]
        raw_next[face * 16 : face * 16 + 16, :] = packed(ends, half // 2, 16)
        raw_prev[face * 16 : face * 16 + 16, :] = packed(ends, half // 2 + EDGE, 16)
    pl.semaphore_wait(barrier, expected)
    posted = []
    copies = [send(0, to_next.at[0], edge_prev, nxt), send(1, to_prev.at[0], edge_next, prv)]
    for face in range(4):
        where = pl.ds(face * FACE_ROWS, FACE_ROWS)
        copies.append(send(2 + face, raw_ref.at[where], far_ref.at[where], coords(sides[face])))
    for face in range(4):
        where = pl.ds(face * 16, 16)
        posted.append(post(6 + face, raw_next.at[where], far_prev.at[where], via_next[face]))
        posted.append(post(10 + face, raw_prev.at[where], far_next.at[where], via_prev[face]))

    for load in inputs[3:]:
        load.wait()
    index_ref[...] = jnp.zeros_like(index_ref)
    code_ref[...] = jnp.zeros_like(code_ref)
    index_ref[0:6, 0:elems] = neigh_ref[...]
    code_ref[0:6, 0:elems] = orient_ref[...]
    choices = []
    for face in range(6):
        local = index_ref[face : face + 1, :] - me * elems
        if face < 4:
            own = jnp.logical_and(local >= 0, local < elems)
            local = jnp.where(own, local, capacity + local + (me - sides[face]) * elems)
        width = capacity * (2 if face < 4 else 1)
        columns = lax.broadcasted_iota(jnp.int32, (width, capacity), 0)
        choices.append(jnp.where(columns == local, 1.0, 0.0).astype(jnp.bfloat16))

    lane = lax.broadcasted_iota(jnp.int32, (1, half), 1)

    def merged(low, high, from_prev, from_next, shift, held):
        groups = -(-low.shape[0] // from_prev.shape[0])
        first = unpacked(from_prev, 0, groups)[0 : low.shape[0]]
        last = unpacked(from_next, elems - half - EDGE, groups)[0 : low.shape[0]]
        low = jnp.where(lane + shift < 0, first, low)
        high = jnp.where(lane + half + shift >= held, last, high)
        return low, high

    for copy in copies[:2]:
        copy.wait()
    low, high = merged(
        view_ref[:, 0:half], view_ref[:, half:], edge_prev[...], edge_next[...], shift, held
    )
    view_ref[:, 0:half] = low
    view_ref[:, half:] = high
    traces_ref[...] = times(send_mat[...], view_ref[0:ROWS, :])

    u = [view_ref[NODES * v : NODES * (v + 1), :] for v in range(5)]
    inverse_density = 1.0 / u[0]
    pressure = pressure_of(u, inverse_density)
    flux = [[] for _ in range(5)]
    for k in range(3):
        velocity = u[1 + k] * inverse_density
        flux[0].append(u[1 + k])
        for j in range(3):
            value = u[1 + j] * velocity
            flux[1 + j].append(value + pressure if j == k else value)
        flux[4].append((u[4] + pressure) * velocity)
    volume = [times(along_mat[...], jnp.concatenate(flux[v], axis=0))[0:NODES] for v in range(5)]
    inside = [times(inside_mat[...], u[v])[0:72].reshape(9, 8, capacity) for v in range(5)]

    for copy in copies[2:]:
        copy.wait()
    for item in posted:
        arrive(item)

    out_ref[...] = jnp.zeros_like(out_ref)
    for face in range(6):
        where = pl.ds((face ^ 1) * FACE_ROWS, FACE_ROWS)
        edge = pl.ds((face ^ 1) * 16, 16)
        block = traces_ref[where, :]
        if face < 4:
            low, high = merged(
                far_ref[where, 0:half], far_ref[where, half:], far_prev[edge, :],
                far_next[edge, :], *range_of(sides[face]),
            )
            block = jnp.concatenate([block, low, high], axis=1)
        pieces = jnp.dot(
            jnp.concatenate(parts_of(block), axis=0), choices[face],
            preferred_element_type=jnp.float32,
        )
        taken = pieces[0:48] + pieces[48:96] + pieces[96:144]
        out_ref[:, face, :] = taken[0:45]

    code = code_ref[...]
    swapped = code >= 4
    flip_p = (code & 1) == 1
    flip_q = (code & 2) == 2
    outside = []
    for v in range(5):
        t = [[out_ref[9 * v + 3 * p + q] for q in range(3)] for p in range(3)]
        t = [[jnp.where(swapped, t[q][p], t[p][q]) if p != q else t[p][q] for q in range(3)] for p in range(3)]
        t = [[jnp.where(flip_p, t[2 - p][q], t[p][q]) if p != 1 else t[p][q] for q in range(3)] for p in range(3)]
        t = [[jnp.where(flip_q, t[p][2 - q], t[p][q]) if q != 1 else t[p][q] for q in range(3)] for p in range(3)]
        outside.append(jnp.stack([t[p][q] for p in range(3) for q in range(3)]))

    face_of = lax.broadcasted_iota(jnp.int32, (1, 8, capacity), 1)
    real = face_of < 6
    outward = jnp.where((face_of & 1) == 1, 1.0, -1.0)
    normal = [jnp.logical_and(face_of >= 2 * k, face_of < 2 * k + 2) for k in range(3)]

    def normal_flux(w):
        inverse_density = 1.0 / w[0]
        pressure = pressure_of(w, inverse_density)
        momentum = jnp.where(normal[0], w[1], jnp.where(normal[1], w[2], w[3]))
        velocity = momentum * inverse_density
        values = [momentum]
        for j in range(3):
            values.append(w[1 + j] * velocity + jnp.where(normal[j], pressure, 0.0))
        values.append((w[4] + pressure) * velocity)
        return values, jnp.abs(velocity) + jnp.sqrt(1.4 * pressure * inverse_density)

    flux_in, speed_in = normal_flux(inside)
    flux_out, speed_out = normal_flux(outside)
    speed = jnp.maximum(speed_in, speed_out)
    for v in range(5):
        term = 1.5 * (outward * (flux_out[v] - flux_in[v]) - speed * (outside[v] - inside[v]))
        term = jnp.where(real, term, 0.0).reshape(72, capacity)
        res_ref[NODES * v : NODES * (v + 1), :] = volume[v] + times(lift_mat[...], term)[0:NODES]

    to_prev[1] = packed(res_ref[:, 0:half], 0, TALL // 4)
    to_next[1] = packed(res_ref[:, half:], elems - half - EDGE, TALL // 4)
    copies = [send(14, to_prev.at[1], res_next, prv), send(15, to_next.at[1], res_prev, nxt)]
    residual_ref[...] = res_ref[0:ROWS, 0:elems]
    for copy in copies:
        copy.wait()
    high = jnp.where(
        lane < elems - half, res_ref[0:ROWS, half:],
        jnp.where(
            lane < elems - half + EDGE,
            unpacked(res_next[...], elems - half, 4)[0:ROWS],
            unpacked(res_prev[...], elems - half + EDGE, 4)[0:ROWS],
        ),
    )
    old_res[...] = pltpu.roll(
        jnp.concatenate([res_ref[0:ROWS, 0:half], high], axis=1), to_old, 1
    )

    for chunk in range(CHUNKS):
        loads[chunk].wait()

        def apply(step, carry):
            for t in range(3):
                row = chunk * rows + step * 3 + t
                product = block_ref[row].astype(jnp.float32) * old_res[...]
                upd_ref[pl.ds(row, 1), :] = jnp.sum(product, axis=0, keepdims=True)
            return carry

        lax.fori_loop(0, rows // 3, apply, 0)

    upd_ref[0:ROWS, :] = pltpu.roll(upd_ref[0:ROWS, :], to_new, 1)
    to_next[2] = packed(upd_ref[:, half:], half // 2, TALL // 4)
    to_prev[2] = packed(upd_ref[:, half:], half // 2 + EDGE, TALL // 4)
    copies = [send(16, to_next.at[2], upd_prev, nxt), send(17, to_prev.at[2], upd_next, prv)]
    for copy in copies:
        copy.wait()
    low, high = merged(
        upd_ref[:, 0:half], upd_ref[:, half:], upd_prev[...], upd_next[...], shift, held
    )
    new_ref[:, 0:half] = (view_ref[:, 0:half] - low)[0:ROWS]
    new_ref[:, half:elems] = (view_ref[:, half:] - high)[0:ROWS, 0 : elems - half]


def solution(mesh):
    n_gx, n_gy = mesh.shape["gx"], mesh.shape["gy"]

    def body(old_state, old_inverse, old_start, neighbours, orientation):
        elems, capacity = neighbours.shape[1], old_state.shape[1]
        half = capacity // 2
        matrices = selections()
        vmem = pl.BlockSpec(memory_space=pltpu.VMEM)
        f32 = lambda *shape: pltpu.VMEM(shape, jnp.float32)
        call = pl.pallas_call(
            lambda *refs: kernel(n_gx, n_gy, *refs),
            out_shape=[jax.ShapeDtypeStruct((ROWS, elems), jnp.float32)] * 2,
            in_specs=[pl.BlockSpec(memory_space=pltpu.HBM)] * 9,
            out_specs=[vmem, vmem],
            scratch_shapes=[
                f32(ROWS, capacity),
                pltpu.SMEM(old_start.shape, jnp.int32),
                pltpu.VMEM((6, elems), jnp.int32), pltpu.VMEM((6, elems), jnp.int32),
                *[pltpu.VMEM(m.shape, m.dtype) for m in matrices],
                pltpu.VMEM((ROWS, ROWS, capacity), jnp.bfloat16),
                f32(TALL, capacity), f32(3, TALL // 4, half), f32(3, TALL // 4, half),
                f32(TALL // 4, half), f32(TALL // 4, half), f32(64, half), f32(64, half),
                f32(4 * FACE_ROWS, capacity), f32(6 * FACE_ROWS, capacity),
                f32(4 * FACE_ROWS, capacity), f32(64, half), f32(64, half),
                f32(45, 8, capacity),
                f32(TALL, capacity), f32(TALL // 4, half), f32(TALL // 4, half),
                f32(ROWS, capacity),
                f32(TALL, capacity), f32(TALL // 4, half), f32(TALL // 4, half),
                pltpu.VMEM((8, capacity), jnp.int32), pltpu.VMEM((8, capacity), jnp.int32),
                pltpu.SemaphoreType.DMA((8,)),
                pltpu.SemaphoreType.DMA((CHUNKS,)),
                pltpu.SemaphoreType.DMA((18,)),
                pltpu.SemaphoreType.DMA((18,)),
            ],
            compiler_params=pltpu.CompilerParams(
                collective_id=0, has_side_effects=True, vmem_limit_bytes=63 * 1024 * 1024
            ),
        )
        return tuple(call(old_state, old_inverse, old_start, neighbours, orientation, *matrices))

    spread = P(None, ("gx", "gy"))
    return jax.shard_map(
        body,
        mesh=mesh,
        in_specs=(spread, P(None, None, ("gx", "gy")), P(), spread, spread),
        out_specs=(spread, spread),
        check_vma=False,
    )
```

```python
import numpy as np
import jax
import jax.numpy as jnp
from jax import lax
from jax.experimental import pallas as pl
from jax.experimental.pallas import tpu as pltpu
from jax.sharding import PartitionSpec as P

DIFF = np.array([[-1.5, 2.0, -0.5], [-0.5, 0.0, 0.5], [0.5, -2.0, 1.5]])
MESH = pl.DeviceIdType.MESH
NODES = 27
ROWS = 135
FACE_ROWS = 48
CHUNKS = 5
TALL = 160
EDGE = 32


def face_node(face, position):
    k, h = face // 2, face % 2
    other = [position // 3, position % 3]
    index = other[:k] + [2 * h] + other[k:]
    return 9 * index[0] + 3 * index[1] + index[2]


def selections():
    send = np.zeros((6 * FACE_ROWS, ROWS), np.float32)
    inside = np.zeros((80, NODES), np.float32)
    lift = np.zeros((32, 72), np.float32)
    for face in range(6):
        for position in range(9):
            node = face_node(face, position)
            for v in range(5):
                send[face * FACE_ROWS + v * 9 + position, v * NODES + node] = 1.0
            inside[position * 8 + face, node] = 1.0
            lift[node, position * 8 + face] = 1.0
    eye = np.eye(3)
    along = np.concatenate(
        [
            np.kron(np.kron(DIFF, eye), eye),
            np.kron(np.kron(eye, DIFF), eye),
            np.kron(np.kron(eye, eye), DIFF),
        ],
        axis=1,
    ).astype(np.float32)
    along = np.pad(along, ((0, 5), (0, 0)))
    thrice = lambda m: np.concatenate([m, m, m], axis=1)
    return [jnp.asarray(thrice(m), jnp.bfloat16) for m in (send, inside, along, lift)]


def parts_of(x):
    high = x.astype(jnp.bfloat16)
    rest = x - high.astype(jnp.float32)
    mid = rest.astype(jnp.bfloat16)
    low = (rest - mid.astype(jnp.float32)).astype(jnp.bfloat16)
    return [high, mid, low]


def times(matrix, x):
    return jnp.dot(
        matrix, jnp.concatenate(parts_of(x), axis=0), preferred_element_type=jnp.float32
    )


def packed(x, first, height):
    lane = lax.broadcasted_iota(jnp.int32, (1, 128), 1)
    result = jnp.zeros((height, 128), x.dtype)
    for group in range(x.shape[0] // height):
        rolled = pltpu.roll(
            x[group * height : (group + 1) * height], (group * EDGE - first) % 128, 1
        )
        inside = jnp.logical_and(lane >= group * EDGE, lane < (group + 1) * EDGE)
        result = jnp.where(inside, rolled, result)
    return result


def unpacked(x, first, groups):
    return jnp.concatenate(
        [pltpu.roll(x, (first - group * EDGE) % 128, 1) for group in range(groups)], axis=0
    )


def pressure_of(u, inverse_density):
    kinetic = (u[1] * u[1] + u[2] * u[2] + u[3] * u[3]) * inverse_density
    return 0.4 * (u[4] - 0.5 * kinetic)


def kernel(
    n_gx, n_gy,
    state_hbm, inverse_ref, start_hbm, neigh_hbm, orient_hbm, send_hbm, inside_hbm, along_hbm, lift_hbm,
    new_ref, residual_ref,
    state_ref, start_ref, neigh_ref, orient_ref, send_mat, inside_mat, along_mat, lift_mat,
    block_ref, view_ref, to_prev, to_next, edge_prev, edge_next, raw_prev, raw_next,
    raw_ref, traces_ref, far_ref, far_prev, far_next, out_ref, res_ref, res_prev, res_next,
    old_res, upd_ref, upd_prev, upd_next, index_ref, code_ref,
    input_sem, load_sem, send_sem, recv_sem,
):
    elems = neigh_ref.shape[1]
    capacity = state_ref.shape[1]
    half = capacity // 2
    count = n_gx * n_gy
    gx = lax.axis_index("gx")
    gy = lax.axis_index("gy")
    me = gx * n_gy + gy

    after = lax.rem(me + 1, count)
    before = lax.rem(me + count - 1, count)
    def coords(device):
        return (device // n_gy, lax.rem(device, n_gy))

    def side(face, device):
        x, y = coords(device)
        step = 1 if face % 2 else -1
        if face < 2:
            x = lax.rem(x + n_gx + step, n_gx)
        else:
            y = lax.rem(y + n_gy + step, n_gy)
        return x * n_gy + y

    nxt, prv = coords(after), coords(before)
    sides = [side(face, me) for face in range(4)]
    via_next = [side(face, after) for face in range(4)]
    via_prev = [side(face, before) for face in range(4)]

    inputs = []
    for slot, (source, target) in enumerate(
        [
            (state_hbm, state_ref), (start_hbm, start_ref), (send_hbm, send_mat),
            (neigh_hbm, neigh_ref), (orient_hbm, orient_ref), (inside_hbm, inside_mat),
            (along_hbm, along_mat), (lift_hbm, lift_mat),
        ]
    ):
        load = pltpu.make_async_copy(source, target, input_sem.at[slot])
        load.start()
        inputs.append(load)

    barrier = pltpu.get_barrier_semaphore()
    for device in [after, before] + sides:
        pl.semaphore_signal(barrier, inc=1, device_id=coords(device), device_id_type=MESH)
    expected = 6
    for face in range(4):
        for sender in (
            lax.rem(sides[face] + count - 1, count), lax.rem(sides[face] + 1, count)
        ):
            expected = expected + jnp.where(sender == me, 0, 1)

            @pl.when(sender != me)
            def _():
                pl.semaphore_signal(barrier, inc=1, device_id=coords(sender), device_id_type=MESH)

    rows = ROWS // CHUNKS
    loads = []
    for chunk in range(CHUNKS):
        where = pl.ds(chunk * rows, rows)
        load = pltpu.make_async_copy(
            inverse_ref.at[where], block_ref.at[where], load_sem.at[chunk]
        )
        load.start()
        loads.append(load)

    def send(slot, source, target, device):
        copy = pltpu.make_async_remote_copy(
            src_ref=source, dst_ref=target, send_sem=send_sem.at[slot],
            recv_sem=recv_sem.at[slot], device_id=device, device_id_type=MESH,
        )
        copy.start()
        return copy

    def post(slot, source, target, device):
        remote = pltpu.make_async_remote_copy(
            src_ref=source, dst_ref=target, send_sem=send_sem.at[slot],
            recv_sem=recv_sem.at[slot], device_id=coords(device), device_id_type=MESH,
        )
        local = pltpu.make_async_copy(source, target, recv_sem.at[slot])
        pl.when(device != me)(remote.start)
        pl.when(device == me)(local.start)
        return device, remote, local

    def arrive(posted):
        device, remote, local = posted
        pl.when(device != me)(remote.wait)
        pl.when(device == me)(local.wait)

    def range_of(device):
        start = start_ref[device]
        end = jnp.where(
            device == count - 1, count * elems, start_ref[lax.rem(device + 1, count)]
        )
        return device * elems - start, end - start

    for load in inputs[:3]:
        load.wait()
    shift, held = range_of(me)
    to_new = jnp.where(shift > 0, capacity - shift, -shift)
    to_old = jnp.where(shift >= 0, shift, capacity + shift)

    for ref in (view_ref, res_ref, upd_ref):
        ref[ROWS:, :] = jnp.zeros((TALL - ROWS, capacity), jnp.float32)
    view_ref[0:ROWS, :] = pltpu.roll(state_ref[...], to_new, 1)
    to_next[0] = packed(view_ref[:, half:], half // 2, TALL // 4)
    to_prev[0] = packed(view_ref[:, half:], half // 2 + EDGE, TALL // 4)
    raw_ref[...] = times(send_mat[pl.ds(0, 4 * FACE_ROWS), :], view_ref[0:ROWS, :])
    for face in range(4):
        ends = raw_ref[face * FACE_ROWS : (face + 1) * FACE_ROWS, half:]
        raw_next[face * 16 : face * 16 + 16, :] = packed(ends, half // 2, 16)
        raw_prev[face * 16 : face * 16 + 16, :] = packed(ends, half // 2 + EDGE, 16)
    pl.semaphore_wait(barrier, expected)
    posted = []
    copies = [send(0, to_next.at[0], edge_prev, nxt), send(1, to_prev.at[0], edge_next, prv)]
    for face in range(4):
        where = pl.ds(face * FACE_ROWS, FACE_ROWS)
        copies.append(send(2 + face, raw_ref.at[where], far_ref.at[where], coords(sides[face])))
    for face in range(4):
        where = pl.ds(face * 16, 16)
        posted.append(post(6 + face, raw_next.at[where], far_prev.at[where], via_next[face]))
        posted.append(post(10 + face, raw_prev.at[where], far_next.at[where], via_prev[face]))

    for load in inputs[3:]:
        load.wait()
    index_ref[...] = jnp.zeros_like(index_ref)
    code_ref[...] = jnp.zeros_like(code_ref)
    index_ref[0:6, 0:elems] = neigh_ref[...]
    code_ref[0:6, 0:elems] = orient_ref[...]
    choices = []
    for face in range(6):
        local = index_ref[face : face + 1, :] - me * elems
        if face < 4:
            own = jnp.logical_and(local >= 0, local < elems)
            local = jnp.where(own, local, capacity + local + (me - sides[face]) * elems)
        width = capacity * (2 if face < 4 else 1)
        columns = lax.broadcasted_iota(jnp.int32, (width, capacity), 0)
        choices.append(jnp.where(columns == local, 1.0, 0.0).astype(jnp.bfloat16))

    lane = lax.broadcasted_iota(jnp.int32, (1, half), 1)

    def merged(low, high, from_prev, from_next, shift, held):
        groups = -(-low.shape[0] // from_prev.shape[0])
        first = unpacked(from_prev, 0, groups)[0 : low.shape[0]]
        last = unpacked(from_next, elems - half - EDGE, groups)[0 : low.shape[0]]
        low = jnp.where(lane + shift < 0, first, low)
        high = jnp.where(lane + half + shift >= held, last, high)
        return low, high

    for copy in copies[:2]:
        copy.wait()
    low, high = merged(
        view_ref[:, 0:half], view_ref[:, half:], edge_prev[...], edge_next[...], shift, held
    )
    view_ref[:, 0:half] = low
    view_ref[:, half:] = high
    traces_ref[...] = times(send_mat[...], view_ref[0:ROWS, :])

    u = [view_ref[NODES * v : NODES * (v + 1), :] for v in range(5)]
    inverse_density = 1.0 / u[0]
    pressure = pressure_of(u, inverse_density)
    flux = [[] for _ in range(5)]
    for k in range(3):
        velocity = u[1 + k] * inverse_density
        flux[0].append(u[1 + k])
        for j in range(3):
            value = u[1 + j] * velocity
            flux[1 + j].append(value + pressure if j == k else value)
        flux[4].append((u[4] + pressure) * velocity)
    volume = [times(along_mat[...], jnp.concatenate(flux[v], axis=0))[0:NODES] for v in range(5)]
    inside = [times(inside_mat[...], u[v])[0:72].reshape(9, 8, capacity) for v in range(5)]

    for copy in copies[2:]:
        copy.wait()
    for item in posted:
        arrive(item)

    out_ref[...] = jnp.zeros_like(out_ref)
    for face in range(6):
        where = pl.ds((face ^ 1) * FACE_ROWS, FACE_ROWS)
        edge = pl.ds((face ^ 1) * 16, 16)
        block = traces_ref[where, :]
        if face < 4:
            low, high = merged(
                far_ref[where, 0:half], far_ref[where, half:], far_prev[edge, :],
                far_next[edge, :], *range_of(sides[face]),
            )
            block = jnp.concatenate([block, low, high], axis=1)
        pieces = jnp.dot(
            jnp.concatenate(parts_of(block), axis=0), choices[face],
            preferred_element_type=jnp.float32,
        )
        taken = pieces[0:48] + pieces[48:96] + pieces[96:144]
        out_ref[:, face, :] = taken[0:45]

    code = code_ref[...]
    swapped = code >= 4
    flip_p = (code & 1) == 1
    flip_q = (code & 2) == 2
    outside = []
    for v in range(5):
        t = [[out_ref[9 * v + 3 * p + q] for q in range(3)] for p in range(3)]
        t = [[jnp.where(swapped, t[q][p], t[p][q]) if p != q else t[p][q] for q in range(3)] for p in range(3)]
        t = [[jnp.where(flip_p, t[2 - p][q], t[p][q]) if p != 1 else t[p][q] for q in range(3)] for p in range(3)]
        t = [[jnp.where(flip_q, t[p][2 - q], t[p][q]) if q != 1 else t[p][q] for q in range(3)] for p in range(3)]
        outside.append(jnp.stack([t[p][q] for p in range(3) for q in range(3)]))

    face_of = lax.broadcasted_iota(jnp.int32, (1, 8, capacity), 1)
    real = face_of < 6
    outward = jnp.where((face_of & 1) == 1, 1.0, -1.0)
    normal = [jnp.logical_and(face_of >= 2 * k, face_of < 2 * k + 2) for k in range(3)]

    def normal_flux(w):
        inverse_density = 1.0 / w[0]
        pressure = pressure_of(w, inverse_density)
        momentum = jnp.where(normal[0], w[1], jnp.where(normal[1], w[2], w[3]))
        velocity = momentum * inverse_density
        values = [momentum]
        for j in range(3):
            values.append(w[1 + j] * velocity + jnp.where(normal[j], pressure, 0.0))
        values.append((w[4] + pressure) * velocity)
        return values, jnp.abs(velocity) + jnp.sqrt(1.4 * pressure * inverse_density)

    flux_in, speed_in = normal_flux(inside)
    flux_out, speed_out = normal_flux(outside)
    speed = jnp.maximum(speed_in, speed_out)
    for v in range(5):
        term = 1.5 * (outward * (flux_out[v] - flux_in[v]) - speed * (outside[v] - inside[v]))
        term = jnp.where(real, term, 0.0).reshape(72, capacity)
        res_ref[NODES * v : NODES * (v + 1), :] = volume[v] + times(lift_mat[...], term)[0:NODES]

    to_prev[1] = packed(res_ref[:, 0:half], 0, TALL // 4)
    to_next[1] = packed(res_ref[:, half:], elems - half - EDGE, TALL // 4)
    copies = [send(14, to_prev.at[1], res_next, prv), send(15, to_next.at[1], res_prev, nxt)]
    residual_ref[...] = res_ref[0:ROWS, 0:elems]
    for copy in copies:
        copy.wait()
    high = jnp.where(
        lane < elems - half, res_ref[0:ROWS, half:],
        jnp.where(
            lane < elems - half + EDGE,
            unpacked(res_next[...], elems - half, 4)[0:ROWS],
            unpacked(res_prev[...], elems - half + EDGE, 4)[0:ROWS],
        ),
    )
    old_res[...] = pltpu.roll(
        jnp.concatenate([res_ref[0:ROWS, 0:half], high], axis=1), to_old, 1
    )

    for chunk in range(CHUNKS):
        loads[chunk].wait()

        def apply(step, carry):
            for t in range(9):
                row = chunk * rows + step * 9 + t
                product = block_ref[row].astype(jnp.float32) * old_res[...]
                upd_ref[pl.ds(row, 1), :] = jnp.sum(product, axis=0, keepdims=True)
            return carry

        lax.fori_loop(0, rows // 9, apply, 0)

    upd_ref[0:ROWS, :] = pltpu.roll(upd_ref[0:ROWS, :], to_new, 1)
    to_next[2] = packed(upd_ref[:, half:], half // 2, TALL // 4)
    to_prev[2] = packed(upd_ref[:, half:], half // 2 + EDGE, TALL // 4)
    copies = [send(16, to_next.at[2], upd_prev, nxt), send(17, to_prev.at[2], upd_next, prv)]
    for copy in copies:
        copy.wait()
    low, high = merged(
        upd_ref[:, 0:half], upd_ref[:, half:], upd_prev[...], upd_next[...], shift, held
    )
    new_ref[:, 0:half] = (view_ref[:, 0:half] - low)[0:ROWS]
    new_ref[:, half:elems] = (view_ref[:, half:] - high)[0:ROWS, 0 : elems - half]


def solution(mesh):
    n_gx, n_gy = mesh.shape["gx"], mesh.shape["gy"]

    def body(old_state, old_inverse, old_start, neighbours, orientation):
        elems, capacity = neighbours.shape[1], old_state.shape[1]
        half = capacity // 2
        matrices = selections()
        vmem = pl.BlockSpec(memory_space=pltpu.VMEM)
        f32 = lambda *shape: pltpu.VMEM(shape, jnp.float32)
        call = pl.pallas_call(
            lambda *refs: kernel(n_gx, n_gy, *refs),
            out_shape=[jax.ShapeDtypeStruct((ROWS, elems), jnp.float32)] * 2,
            in_specs=[pl.BlockSpec(memory_space=pltpu.HBM)] * 9,
            out_specs=[vmem, vmem],
            scratch_shapes=[
                f32(ROWS, capacity),
                pltpu.SMEM(old_start.shape, jnp.int32),
                pltpu.VMEM((6, elems), jnp.int32), pltpu.VMEM((6, elems), jnp.int32),
                *[pltpu.VMEM(m.shape, m.dtype) for m in matrices],
                pltpu.VMEM((ROWS, ROWS, capacity), jnp.bfloat16),
                f32(TALL, capacity), f32(3, TALL // 4, half), f32(3, TALL // 4, half),
                f32(TALL // 4, half), f32(TALL // 4, half), f32(64, half), f32(64, half),
                f32(4 * FACE_ROWS, capacity), f32(6 * FACE_ROWS, capacity),
                f32(4 * FACE_ROWS, capacity), f32(64, half), f32(64, half),
                f32(45, 8, capacity),
                f32(TALL, capacity), f32(TALL // 4, half), f32(TALL // 4, half),
                f32(ROWS, capacity),
                f32(TALL, capacity), f32(TALL // 4, half), f32(TALL // 4, half),
                pltpu.VMEM((8, capacity), jnp.int32), pltpu.VMEM((8, capacity), jnp.int32),
                pltpu.SemaphoreType.DMA((8,)),
                pltpu.SemaphoreType.DMA((CHUNKS,)),
                pltpu.SemaphoreType.DMA((18,)),
                pltpu.SemaphoreType.DMA((18,)),
            ],
            compiler_params=pltpu.CompilerParams(
                collective_id=0, has_side_effects=True, vmem_limit_bytes=63 * 1024 * 1024
            ),
        )
        return tuple(call(old_state, old_inverse, old_start, neighbours, orientation, *matrices))

    spread = P(None, ("gx", "gy"))
    return jax.shard_map(
        body,
        mesh=mesh,
        in_specs=(spread, P(None, None, ("gx", "gy")), P(), spread, spread),
        out_specs=(spread, spread),
        check_vma=False,
    )
```
